512 devices in a mesh: dp: 64 (over x, z_hi, y, core), fsdp: 8 (over z_lo).
Axes of the slice: x: 4, y: 4, z: 16 (z_hi: 2, z_lo: 8; z = z_hi * 8 + z_lo), core: 2. Of those that a mesh axis runs over, the one named last changes fastest.
Arguments:
- image_features: bfloat16 [196608, 1152], P(('dp', 'fsdp')), may hold values from -24 to 24
- head_weight: bfloat16 [1152, 1152], P('fsdp'), may hold values from -0.0048828125 to 0.0048828125
- text_embeds: bfloat16 [196608, 1152], P(('dp', 'fsdp')), may hold values from -0.17675781 to 0.17675781
- partner: int32 [196608], P(('dp', 'fsdp')), may hold values from 0 to 196607, as said below
- logit_scale: float32 [1], replicated, may hold values from 1.5 to 2.5
- logit_bias: float32 [1], replicated, may hold values from -4 to -1
Outputs:
- text_grad: bfloat16 [196608, 1152], P(('dp', 'fsdp'))
- head_grad: float32 [1152, 1152], P('fsdp')
The draws below stay inside these ranges and needn't reach their ends.
Inputs may be any that keep to these rules, and one draw needn't show every extreme that they name: The partner of an image in block (p, q) is a text of block ((p + k) mod 64, q) for some k from 0 to 3.
All inputs are finite; a program needn't handle non-finite values.
Results may differ from the reference program's by a relative error of at most 0.015.
Values may be sent and summed in bfloat16 or wider, within the bound.
No kernel may reach another device: no remote copies, remote signals or barrier semaphores. Data moves between devices by JAX's collectives and lax.ppermute only.
A program may use at most 64 MiB of HBM per device.

```python
import jax
import jax.numpy as jnp
from jax import lax

D = 1152
E = 1152
ROWS = 384
STEPS = 4
TOKENS = 196608
N_DP = 64
N_FSDP = 8


def draw_partner(key, part):
    key = jax.random.fold_in(key, 7)
    first, second = jax.random.split(key)
    rows_all = jnp.arange(TOKENS, dtype=jnp.int32)
    block = rows_all // ROWS
    place = block // N_FSDP
    lane = block % N_FSDP
    ahead = jax.random.randint(first, (TOKENS,), 0, STEPS, dtype=jnp.int32)
    offset = jax.random.randint(second, (TOKENS,), 0, ROWS, dtype=jnp.int32)
    ahead = jnp.where((rows_all == 0) | (rows_all == TOKENS - 1), 0, ahead).astype(jnp.int32)
    offset = jnp.where(rows_all == 0, 0, offset)
    offset = jnp.where(rows_all == TOKENS - 1, ROWS - 1, offset).astype(jnp.int32)
    return (((place + ahead) % N_DP * N_FSDP + lane) * ROWS + offset).astype(jnp.int32)


def raised(result, rng, source, target, blocks, factor):
    def block_of(position):
        return (jnp.arange(result.shape[position]) // (result.shape[position] // blocks)).reshape((-1,) + (1,) * (result.ndim - 1 - position))

    first = jax.random.permutation(rng, blocks)[block_of(target)]
    second = (block_of(target) + blocks // 2) % blocks
    return jnp.where((block_of(source) == first) | (block_of(source) == second), factor * result, result)


def shard_levels(stream_key, dims, pieces, least, high):
    loudness, own = 1.0, jax.random.fold_in(stream_key, 6)
    for position, shards_of in pieces:
        heights = jnp.exp(jax.random.uniform(jax.random.fold_in(own, position), (shards_of,), jnp.float32, least / len(pieces), high / len(pieces)))
        loudness = loudness * jnp.repeat(heights, dims[position] // shards_of).reshape([-1 if axis == position else 1 for axis in range(len(dims))])
    return loudness


def gaussian(own_key, extent, scale, bound, shards=(), kind=jnp.bfloat16):
    values = scale * jax.random.normal(own_key, extent, jnp.float32)
    if shards:
        values = values * shard_levels(own_key, extent, shards, -0.22, 0.18)
    return jnp.clip(values, -bound, bound).astype(kind)


def bell_draw_with(own_key, extent, scale, limit, pieces, heavy, kind=jnp.bfloat16):
    values = scale * jax.random.normal(own_key, extent, jnp.float32)
    if pieces:
        values = values * shard_levels(own_key, extent, pieces, -0.22, 0.18)
    return jnp.clip(raised(values, jax.random.fold_in(own_key, 3), *heavy), -limit, limit).astype(kind)


def setup_inputs(seed: int = 0) -> dict:
    keys = jax.random.split(jax.random.key(seed), 7)
    image_features = bell_draw_with(keys[0], (TOKENS, D), 1.0, 24.0, ((0, 512),), (0, 1, 128, 5.5))
    head_weight = gaussian(keys[1], (D, E), (D * E) ** -0.5, 0.0048828125, ((0, 8),))
    text_embeds = gaussian(keys[2], (TOKENS, E), (E ** -0.5), 0.17675781, ((0, 512),))
    partner = draw_partner(jax.random.fold_in(keys[6], 71), 0)
    logit_scale = jnp.clip(jax.random.uniform(keys[4], (1,), jnp.float32, 1.5, 2.5), 1.5, 2.5)
    logit_bias = jnp.clip(jax.random.uniform(keys[5], (1,), jnp.float32, -4.0, -1.0), -4.0, -1.0)
    return dict(image_features=image_features, head_weight=head_weight, text_embeds=text_embeds, partner=partner, logit_scale=logit_scale, logit_bias=logit_bias)


def reference(image_features, head_weight, text_embeds, partner, logit_scale, logit_bias):
    projected = jnp.dot(image_features, head_weight, preferred_element_type=jnp.float32)
    img_norm = jnp.sqrt(lax.optimization_barrier(jnp.sum(projected * projected, axis=1, keepdims=True)) + 1e-06)
    unit_f = projected / img_norm
    unit_img = unit_f.astype(jnp.bfloat16)
    text_f = text_embeds.astype(jnp.float32)
    txt_norm = jnp.sqrt(lax.optimization_barrier(jnp.sum(text_f * text_f, axis=1, keepdims=True)) + 1e-06)
    unit_t = text_f / txt_norm
    unit_txt = unit_t.astype(jnp.bfloat16)
    scale = jnp.exp(logit_scale[0])
    bias = logit_bias[0]
    img_blocks = unit_img.astype(jnp.float32).reshape(N_DP, N_FSDP, ROWS, E)
    txt_blocks = unit_txt.astype(jnp.float32).reshape(N_DP, N_FSDP, ROWS, E)
    owners = jnp.arange(TOKENS, dtype=jnp.int32).reshape(N_DP, N_FSDP, ROWS)
    pairs = partner.reshape(N_DP, N_FSDP, ROWS)
    img_grad = jnp.zeros((N_DP, N_FSDP, ROWS, E), jnp.float32)
    txt_grad = jnp.zeros((N_DP, N_FSDP, ROWS, E), jnp.float32)
    for ahead in range(STEPS):
        met = jnp.roll(txt_blocks, -ahead, axis=0)
        met_ids = jnp.roll(owners, -ahead, axis=0)
        logits = scale * jnp.einsum('pqie,pqje->pqij', img_blocks, met) + bias
        sign = jnp.where(pairs[..., :, None] == met_ids[..., None, :], 1.0, -1.0)
        weights = (-sign * jax.nn.sigmoid(-sign * logits)).astype(jnp.bfloat16).astype(jnp.float32)
        img_grad = img_grad + scale * jnp.einsum('pqij,pqje->pqie', weights, met)
        part = scale * jnp.einsum('pqij,pqie->pqje', weights, img_blocks)
        txt_grad = txt_grad + jnp.roll(part, ahead, axis=0)
    img_grad = img_grad.reshape(TOKENS, E)
    txt_grad = txt_grad.reshape(TOKENS, E)
    proj_grad = ((img_grad - unit_f * lax.optimization_barrier(jnp.sum(unit_f * img_grad, axis=1, keepdims=True))) / img_norm).astype(jnp.bfloat16)
    text_grad = ((txt_grad - unit_t * lax.optimization_barrier(jnp.sum(unit_t * txt_grad, axis=1, keepdims=True))) / txt_norm).astype(jnp.bfloat16)
    feat_blocks = image_features.reshape(N_DP * N_FSDP, ROWS, D)
    grad_blocks = proj_grad.reshape(N_DP * N_FSDP, ROWS, E)

    def accumulate(total, block):
        feats, grads = block
        term = jnp.dot(feats.T, grads, preferred_element_type=jnp.float32).astype(jnp.bfloat16)
        term = lax.optimization_barrier(term)
        return (total + term.astype(jnp.float32), None)
    head_grad, unused = lax.scan(accumulate, jnp.zeros((D, E), jnp.float32), (feat_blocks, grad_blocks))
    return (text_grad, head_grad)
```

```python
import jax
import jax.numpy as jnp
from jax import lax
from jax.sharding import PartitionSpec as P

STEPS = 4
SIDE = 4
CORES = 2
GROUP = SIDE * CORES
AXES = ("dp", "fsdp")


def along_chain(block, width, lanes, moves):
    groups = width // GROUP
    route = [
        ((g * GROUP + s) * lanes + q, ((g + dg) % groups * GROUP + t) * lanes + q)
        for g in range(groups)
        for q in range(lanes)
        for s, dg, t in moves
    ]
    return lax.ppermute(block, AXES, route)


def by_coords(block, width, lanes, target):
    route = []
    for p in range(width):
        for q in range(lanes):
            x, hi, y, core = p // 16, p // 8 % 2, p // 2 % 4, p % 2
            x2, hi2, y2, core2, q2 = target(x, hi, y, core, q)
            route.append((p * lanes + q, (((x2 * 2 + hi2) * 4 + y2) * 2 + core2) * lanes + q2))
    return lax.ppermute(block, AXES, route)


def on_device(image_features, head_weight, text_embeds, partner, logit_scale, logit_bias):
    bf16, f32 = jnp.bfloat16, jnp.float32
    rows = image_features.shape[0]
    depth = image_features.shape[1]
    width_dp = lax.axis_size("dp")
    lanes = lax.axis_size("fsdp")
    place = lax.axis_index("dp")
    lane = lax.axis_index("fsdp")
    slot = place % GROUP
    core = place % CORES
    at_y = place // CORES % SIDE
    at_x = place // (2 * GROUP)
    first, last = slot == 0, slot == GROUP - 1

    def chain(block, moves):
        return along_chain(block, width_dp, lanes, moves)

    def coords(block, target):
        return by_coords(block, width_dp, lanes, target)

    def core_swap(block):
        return coords(block, lambda x, hi, y, c, q: (x, hi, y, 1 - c, q))

    def x_shift(block, d):
        return coords(block, lambda x, hi, y, c, q: ((x + d) % SIDE, hi, y, c, q))

    def y_shift(block, d):
        return coords(block, lambda x, hi, y, c, q: (x, hi, (y + d) % SIDE, c, q))

    def z_flip(block, bit):
        return coords(block, lambda x, hi, y, c, q: (x, hi, y, c, q ^ bit))

    def hi_flip(block):
        return coords(block, lambda x, hi, y, c, q: (x, 1 - hi, y, c, q))

    held = head_weight.shape[0]
    half = held // CORES
    step = (half // SIDE) // 8 * 8
    window = half - (SIDE - 1) * step

    def weight():
        mine = lax.dynamic_slice_in_dim(head_weight, core * half + at_x * step, window, 0)
        mine = lax.all_gather(mine, "fsdp", axis=0, tiled=False)
        others = [x_shift(mine, d) for d in range(1, SIDE)]
        ours = jnp.zeros((lanes, half, head_weight.shape[1]), bf16)
        for d, piece in enumerate([mine] + others):
            at = (at_x - d) % SIDE * step
            ours = lax.dynamic_update_slice_in_dim(ours, piece, at, 1)
        theirs = core_swap(ours)
        low = jnp.where(core == 0, ours, theirs)
        high = jnp.where(core == 0, theirs, ours)
        return jnp.concatenate([low, high], axis=1).reshape(lanes * held, -1)

    text_f = text_embeds.astype(f32)
    txt_norm = jnp.sqrt(jnp.sum(text_f * text_f, axis=1, keepdims=True) + 1e-06)
    unit_t = text_f / txt_norm
    unit_txt = unit_t.astype(bf16)
    down = [(s, 0, s - 1) for s in range(1, GROUP)]
    up = [(s, 0, s + 1) for s in range(GROUP - 1)]

    far = chain(unit_txt, [(0, -1, 0), (2, -1, 2), (1, 0, 7)])
    full_weight = weight()
    far_2 = chain(far, [(7, -1, 7), (2, 0, 0)])
    text_1 = chain(jnp.where(first, far, unit_txt), down + [(0, 0, 7)])
    got_2 = chain(jnp.where(first, far_2, text_1), down + [(0, 0, 7)])
    text_2 = jnp.where(last, far_2, got_2)
    got_3 = chain(text_2, down)
    text_3 = jnp.where(last, got_2, got_3)
    texts = [unit_txt, text_1, text_2, text_3]

    projected = jnp.dot(image_features, full_weight, preferred_element_type=f32)
    img_norm = jnp.sqrt(jnp.sum(projected * projected, axis=1, keepdims=True) + 1e-06)
    unit_f = projected / img_norm
    unit_img = unit_f.astype(bf16)

    offset = partner % rows
    ahead = (partner // (rows * lanes) - place) % width_dp
    code = jnp.concatenate([ahead, offset // 128, offset % 128]).astype(bf16)
    code = jnp.pad(code, (0, unit_img.shape[1] - code.shape[0]))
    code = jnp.pad(code[None, :], ((0, 7), (0, 0)))
    parcel = jnp.concatenate([unit_img, code], axis=0)

    back = chain(parcel, [(7, 1, 7), (5, 1, 5), (6, 0, 0)])
    back_2 = chain(back, [(0, 1, 0), (5, 0, 7)])
    image_1 = chain(jnp.where(last, back, parcel), up + [(7, 0, 0)])
    come_2 = chain(jnp.where(last, back_2, image_1), up + [(7, 0, 0)])
    image_2 = jnp.where(first, back_2, come_2)
    come_3 = chain(image_2, up)
    image_3 = jnp.where(first, come_2, come_3)

    scale = jnp.exp(logit_scale[0])
    bias = logit_bias[0]
    offsets = lax.iota(jnp.int32, rows)

    def pair_weight(logits, match):
        sign = jnp.where(match, 1.0, -1.0)
        return (-sign * jax.nn.sigmoid(-sign * logits)).astype(bf16)

    img_grad = 0.0
    for k, text in enumerate(texts):
        logits = scale * jnp.einsum("ie,je->ij", unit_img, text, preferred_element_type=f32) + bias
        met = jnp.where(ahead == k, offset, -1)
        weights = pair_weight(logits, met[:, None] == offsets[None, :])
        img_grad = img_grad + scale * jnp.dot(weights, text, preferred_element_type=f32)
    proj_grad = (
        (img_grad - unit_f * jnp.sum(unit_f * img_grad, axis=1, keepdims=True)) / img_norm
    ).astype(bf16)

    term = jnp.einsum(
        "rd,re->de", image_features, proj_grad, preferred_element_type=f32
    ).astype(bf16)
    cols = term.shape[1]
    term = term.reshape(lanes, CORES, half, cols)
    ours = lax.dynamic_index_in_dim(term, core, 1, keepdims=False)
    theirs = lax.dynamic_index_in_dim(term, 1 - core, 1, keepdims=False)
    total = ours.astype(f32) + core_swap(theirs).astype(f32)

    def cut_x(d):
        return lax.dynamic_slice_in_dim(total, (at_x + d) % SIDE * step, window, 1)

    sent = [x_shift(cut_x(d).astype(bf16), d) for d in range(1, SIDE)]
    total_x = cut_x(0)
    for piece in sent:
        total_x = total_x + piece.astype(f32)
    step_y = (cols // SIDE) // 128 * 128
    window_y = cols - (SIDE - 1) * step_y

    def cut_y(d):
        return lax.dynamic_slice_in_dim(total_x, (at_y + d) % SIDE * step_y, window_y, 2)

    sent = [y_shift(cut_y(d).astype(bf16), d) for d in range(1, SIDE)]
    total_z = cut_y(0)
    for piece in sent:
        total_z = total_z + piece.astype(f32)
    bit = lanes // 2
    while bit:
        halves = total_z.reshape(2, bit, window, window_y)
        side = lane // bit % 2
        keep = lax.dynamic_index_in_dim(halves, side, 0, keepdims=False)
        give = lax.dynamic_index_in_dim(halves, 1 - side, 0, keepdims=False)
        total_z = keep + z_flip(give.astype(bf16), bit).astype(f32)
        bit //= 2
    total_z = total_z.reshape(window, window_y)
    total_z = (total_z + hi_flip(total_z)).astype(bf16)

    pieces = [total_z] + [y_shift(total_z, d) for d in range(1, SIDE)]
    strip = jnp.zeros((window, cols), bf16)
    for d, piece in enumerate(pieces):
        strip = lax.dynamic_update_slice_in_dim(strip, piece, (at_y - d) % SIDE * step_y, 1)
    pieces = [strip] + [x_shift(strip, d) for d in range(1, SIDE)]
    ours = jnp.zeros((half, cols), bf16)
    for d, piece in enumerate(pieces):
        ours = lax.dynamic_update_slice_in_dim(ours, piece, (at_x - d) % SIDE * step, 0)
    theirs = core_swap(ours)
    low = jnp.where(core == 0, ours, theirs)
    high = jnp.where(core == 0, theirs, ours)
    head_grad = jnp.concatenate([low, high], axis=0).astype(f32)

    txt_grad = 0.0
    for k, image in enumerate([parcel, image_1, image_2, image_3]):
        unit, marks = image[:rows], image[rows].astype(f32).astype(jnp.int32)
        met = marks[rows : 2 * rows] * 128 + marks[2 * rows : 3 * rows]
        met = jnp.where(marks[:rows] == k, met, -1)
        logits = scale * jnp.einsum("je,ie->ji", unit_txt, unit, preferred_element_type=f32) + bias
        weights = pair_weight(logits, met[None, :] == offsets[:, None])
        txt_grad = txt_grad + scale * jnp.dot(weights, unit, preferred_element_type=f32)
    text_grad = (
        (txt_grad - unit_t * jnp.sum(unit_t * txt_grad, axis=1, keepdims=True)) / txt_norm
    ).astype(bf16)
    return (text_grad, head_grad)


def solution(mesh):
    in_specs = (
        P(("dp", "fsdp"), None),
        P("fsdp", None),
        P(("dp", "fsdp"), None),
        P(("dp", "fsdp")),
        P(),
        P(),
    )
    out_specs = (P(("dp", "fsdp"), None), P("fsdp", None))
    return jax.shard_map(
        on_device, mesh=mesh, in_specs=in_specs, out_specs=out_specs, check_vma=False
    )
```

```python
import jax
import jax.numpy as jnp
from jax import lax
from jax.sharding import PartitionSpec as P

STEPS = 4
SIDE = 4
CORES = 2
GROUP = SIDE * CORES
AXES = ("dp", "fsdp")


def along_chain(block, width, lanes, moves):
    groups = width // GROUP
    route = [
        ((g * GROUP + s) * lanes + q, ((g + dg) % groups * GROUP + t) * lanes + q)
        for g in range(groups)
        for q in range(lanes)
        for s, dg, t in moves
    ]
    return lax.ppermute(block, AXES, route)


def by_coords(block, width, lanes, target):
    route = []
    for p in range(width):
        for q in range(lanes):
            x, hi, y, core = p // 16, p // 8 % 2, p // 2 % 4, p % 2
            x2, hi2, y2, core2, q2 = target(x, hi, y, core, q)
            route.append((p * lanes + q, (((x2 * 2 + hi2) * 4 + y2) * 2 + core2) * lanes + q2))
    return lax.ppermute(block, AXES, route)


def on_device(image_features, head_weight, text_embeds, partner, logit_scale, logit_bias):
    bf16, f32 = jnp.bfloat16, jnp.float32
    rows = image_features.shape[0]
    depth = image_features.shape[1]
    width_dp = lax.axis_size("dp")
    lanes = lax.axis_size("fsdp")
    place = lax.axis_index("dp")
    lane = lax.axis_index("fsdp")
    slot = place % GROUP
    core = place % CORES
    at_y = place // CORES % SIDE
    at_x = place // (2 * GROUP)
    first, last = slot == 0, slot == GROUP - 1

    def chain(block, moves):
        return along_chain(block, width_dp, lanes, moves)

    def coords(block, target):
        return by_coords(block, width_dp, lanes, target)

    def core_swap(block):
        return coords(block, lambda x, hi, y, c, q: (x, hi, y, 1 - c, q))

    def x_shift(block, d):
        return coords(block, lambda x, hi, y, c, q: ((x + d) % SIDE, hi, y, c, q))

    def y_shift(block, d):
        return coords(block, lambda x, hi, y, c, q: (x, hi, (y + d) % SIDE, c, q))

    def x_flip(block, bit):
        return coords(block, lambda x, hi, y, c, q: (x ^ bit, hi, y, c, q))

    def y_flip(block, bit):
        return coords(block, lambda x, hi, y, c, q: (x, hi, y ^ bit, c, q))

    def z_flip(block, bit):
        return coords(block, lambda x, hi, y, c, q: (x, hi, y, c, q ^ bit))

    def hi_flip(block):
        return coords(block, lambda x, hi, y, c, q: (x, 1 - hi, y, c, q))

    held, cols = head_weight.shape
    half = held // CORES
    step = (half // SIDE) // 8 * 8
    window = half - (SIDE - 1) * step
    step_y = (cols // SIDE) // 128 * 128
    window_y = cols - (SIDE - 1) * step_y

    def in_order(mine, theirs, bit, axis):
        low = jnp.where(bit == 0, mine, theirs)
        high = jnp.where(bit == 0, theirs, mine)
        return jnp.concatenate([low, high], axis=axis)

    scale = jnp.exp(logit_scale[0])
    bias = logit_bias[0]

    def one_step(stage, *blocks):
        def unused(*_):
            return jax.tree.map(lambda r: jnp.zeros(r.shape, r.dtype), jax.eval_shape(stage, *blocks))

        return lax.cond(scale > 0.0, stage, unused, *blocks)

    def gather_z(mine):
        bit = 1
        while bit < lanes:
            mine = in_order(mine, z_flip(mine, bit), lane // bit % 2, 0)
            bit *= 2
        return mine

    def gather_rest(mine):
        pieces = [mine] + [y_shift(mine, d) for d in range(1, SIDE)]
        strip = jnp.zeros((lanes, window, cols), bf16)
        for d, piece in enumerate(pieces):
            strip = lax.dynamic_update_slice_in_dim(strip, piece, (at_y - d) % SIDE * step_y, 2)
        pieces = [strip] + [x_shift(strip, d) for d in range(1, SIDE)]
        ours = jnp.zeros((lanes, half, cols), bf16)
        for d, piece in enumerate(pieces):
            ours = lax.dynamic_update_slice_in_dim(ours, piece, (at_x - d) % SIDE * step, 1)
        return in_order(ours, core_swap(ours), core, 1).reshape(lanes * held, cols)

    def sum_xy(total):
        def cut_x(d):
            return lax.dynamic_slice_in_dim(total, (at_x + d) % SIDE * step, window, 1)

        sent = [x_shift(cut_x(d).astype(bf16), d) for d in range(1, SIDE)]
        total_x = cut_x(0)
        for piece in sent:
            total_x = total_x + piece.astype(f32)

        def cut_y(d):
            return lax.dynamic_slice_in_dim(total_x, (at_y + d) % SIDE * step_y, window_y, 2)

        sent = [y_shift(cut_y(d).astype(bf16), d) for d in range(1, SIDE)]
        total_y = cut_y(0)
        for piece in sent:
            total_y = total_y + piece.astype(f32)
        return total_y

    text_f = text_embeds.astype(f32)
    txt_norm = jnp.sqrt(jnp.sum(text_f * text_f, axis=1, keepdims=True) + 1e-06)
    unit_t = text_f / txt_norm
    unit_txt = unit_t.astype(bf16)
    down = [(s, 0, s - 1) for s in range(1, GROUP)]
    up = [(s, 0, s + 1) for s in range(GROUP - 1)]

    far = chain(unit_txt, [(0, -1, 7), (2, -1, 2)])
    ready, _ = lax.optimization_barrier((head_weight, unit_txt))
    mine = lax.dynamic_slice(
        ready, (core * half + at_x * step, at_y * step_y), (window, window_y)
    )[None]

    def gather(mine):
        mine, moved, near = one_step(
            lambda m: (gather_z(m), chain(unit_txt, [(1, 0, 6)]), chain(unit_txt, down)), mine
        )
        far_1 = chain(moved, [(6, -1, 6)])
        whole = one_step(gather_rest, mine)
        return *lax.optimization_barrier((whole, far_1)), near

    full_weight, far_1, near = one_step(gather, mine)
    full_weight, far = lax.optimization_barrier((full_weight, far))

    projected = jnp.dot(image_features, full_weight, preferred_element_type=f32)
    img_norm = jnp.sqrt(jnp.sum(projected * projected, axis=1, keepdims=True) + 1e-06)
    unit_f = projected / img_norm
    unit_img = unit_f.astype(bf16)

    offset = partner % rows
    ahead = (partner // (rows * lanes) - place) % width_dp
    code = jnp.concatenate([ahead, offset // 128, offset % 128]).astype(bf16)
    code = jnp.pad(code, (0, unit_img.shape[1] - code.shape[0]))
    code = jnp.pad(code[None, :], ((0, 7), (0, 0)))
    parcel = jnp.concatenate([unit_img, code], axis=0)

    back = chain(parcel, [(7, 1, 0), (5, 1, 5)])

    offsets = lax.iota(jnp.int32, rows)

    def pair_weight(logits, match):
        sign = jnp.where(match, 1.0, -1.0)
        weights = (-sign * jax.nn.sigmoid(-sign * logits)).astype(bf16)
        return lax.optimization_barrier(weights)

    def met_grad(text, k):
        logits = jnp.einsum("ie,je->ij", unit_img, text, preferred_element_type=f32)
        met = jnp.where(ahead == k, offset, -1)
        weights = pair_weight(scale * logits + bias, met[:, None] == offsets[None, :])
        return scale * jnp.dot(weights, text, preferred_element_type=f32)

    def meet_texts(far, near, far_1):
        far_2 = chain(far, [(2, 0, 7)])
        text_1 = jnp.where(last, far, near)
        text_2 = chain(text_1, down)
        text_3 = chain(text_2, down)
        far_3 = chain(far_1, [(6, 0, 7)])
        text_2 = jnp.where(last, far_2, text_2)
        text_3 = jnp.where(last, far_3, jnp.where(slot == GROUP - 2, far_1, text_3))
        texts = [
            (unit_txt, 0),
            (text_1, 1),
            (text_2, jnp.where(last, 3, 2)),
            (text_3, jnp.where(last, 2, 3)),
        ]
        img_grad = 0.0
        for text, k in texts[:-1]:
            img_grad = img_grad + met_grad(text, k)
        back_0 = chain(parcel, [(6, 0, 1)])
        return img_grad, text_3, back_0, chain(parcel, up)

    def head_terms(img_grad, text):
        img_grad = img_grad + met_grad(text, jnp.where(last, 2, 3))
        proj_grad = (
            (img_grad - unit_f * jnp.sum(unit_f * img_grad, axis=1, keepdims=True)) / img_norm
        ).astype(bf16)
        term = jnp.einsum(
            "rd,re->de", image_features, proj_grad, preferred_element_type=f32
        ).astype(bf16)
        term = term.reshape(lanes, CORES, half, cols)
        ours = lax.dynamic_index_in_dim(term, core, 1, keepdims=False)
        theirs = lax.dynamic_index_in_dim(term, 1 - core, 1, keepdims=False)
        return ours.astype(f32) + core_swap(theirs).astype(f32)

    def sum_z(total):
        bit = lanes // 2
        while bit:
            halves = total.reshape(2, bit, window, window_y)
            side = lane // bit % 2
            keep = lax.dynamic_index_in_dim(halves, side, 0, keepdims=False)
            give = lax.dynamic_index_in_dim(halves, 1 - side, 0, keepdims=False)
            total = keep + z_flip(give.astype(bf16), bit).astype(f32)
            bit //= 2
        total = total.reshape(window, window_y)
        return (total + hi_flip(total)).astype(bf16)

    img_grad, text, back_0, beside = one_step(meet_texts, far, near, far_1)
    back_1 = chain(back_0, [(1, 1, 1)])
    total = one_step(lambda *blocks: sum_xy(head_terms(*blocks)), img_grad, text)
    total, back, back_1 = lax.optimization_barrier((total, back, back_1))
    back_2 = chain(back, [(5, 0, 0)])
    image_1 = jnp.where(first, back, beside)
    image_2 = chain(image_1, up)
    total_z = one_step(sum_z, total)
    total_z, back_2, image_2, parcel, image_1 = lax.optimization_barrier(
        (total_z, back_2, image_2, parcel, image_1)
    )
    image_3 = chain(image_2, up)
    back_3 = chain(back_1, [(1, 0, 0)])
    image_2 = jnp.where(first, back_2, image_2)
    image_3 = jnp.where(first, back_3, jnp.where(slot == 1, back_1, image_3))

    strips = total_z[None]
    for bit in (1, 2):
        strips = in_order(strips, y_flip(strips, bit), at_y // bit % 2, 0)
    strip = jnp.concatenate(
        [strips[j, :, :step_y] for j in range(SIDE - 1)] + [strips[SIDE - 1]], axis=1
    )[None]
    for bit in (1, 2):
        strip = in_order(strip, x_flip(strip, bit), at_x // bit % 2, 0)
    ours = jnp.concatenate(
        [strip[j, :step] for j in range(SIDE - 1)] + [strip[SIDE - 1]], axis=0
    )
    head_grad = in_order(ours, core_swap(ours), core, 0).astype(f32)

    images = [
        (parcel, 0),
        (image_1, 1),
        (image_2, jnp.where(first, 3, 2)),
        (image_3, jnp.where(first, 2, 3)),
    ]

    txt_grad = 0.0
    for image, k in images:
        unit, marks = image[:rows], image[rows].astype(f32).astype(jnp.int32)
        met = marks[rows : 2 * rows] * 128 + marks[2 * rows : 3 * rows]
        met = jnp.where(marks[:rows] == k, met, -1)
        logits = scale * jnp.einsum("je,ie->ji", unit_txt, unit, preferred_element_type=f32) + bias
        weights = pair_weight(logits, met[None, :] == offsets[:, None])
        txt_grad = txt_grad + scale * jnp.dot(weights, unit, preferred_element_type=f32)
    text_grad = (
        (txt_grad - unit_t * jnp.sum(unit_t * txt_grad, axis=1, keepdims=True)) / txt_norm
    ).astype(bf16)
    return (text_grad, head_grad)


def solution(mesh):
    in_specs = (
        P(("dp", "fsdp"), None),
        P("fsdp", None),
        P(("dp", "fsdp"), None),
        P(("dp", "fsdp")),
        P(),
        P(),
    )
    out_specs = (P(("dp", "fsdp"), None), P("fsdp", None))
    return jax.shard_map(
        on_device, mesh=mesh, in_specs=in_specs, out_specs=out_specs, check_vma=False
    )
```

```python
import jax
import jax.numpy as jnp
from jax import lax
from jax.sharding import PartitionSpec as P

STEPS = 4
SIDE = 4
CORES = 2
GROUP = SIDE * CORES
AXES = ("dp", "fsdp")


def along_chain(block, width, lanes, moves):
    groups = width // GROUP
    route = [
        ((g * GROUP + s) * lanes + q, ((g + dg) % groups * GROUP + t) * lanes + q)
        for g in range(groups)
        for q in range(lanes)
        for s, dg, t in moves
    ]
    return lax.ppermute(block, AXES, route)


def by_coords(block, width, lanes, target):
    route = []
    for p in range(width):
        for q in range(lanes):
            x, hi, y, core = p // 16, p // 8 % 2, p // 2 % 4, p % 2
            x2, hi2, y2, core2, q2 = target(x, hi, y, core, q)
            route.append((p * lanes + q, (((x2 * 2 + hi2) * 4 + y2) * 2 + core2) * lanes + q2))
    return lax.ppermute(block, AXES, route)


def on_device(image_features, head_weight, text_embeds, partner, logit_scale, logit_bias):
    bf16, f32 = jnp.bfloat16, jnp.float32
    rows = image_features.shape[0]
    depth = image_features.shape[1]
    width_dp = lax.axis_size("dp")
    lanes = lax.axis_size("fsdp")
    place = lax.axis_index("dp")
    lane = lax.axis_index("fsdp")
    slot = place % GROUP
    core = place % CORES
    at_y = place // CORES % SIDE
    at_x = place // (2 * GROUP)
    first, last = slot == 0, slot == GROUP - 1

    def chain(block, moves):
        return along_chain(block, width_dp, lanes, moves)

    def coords(block, target):
        return by_coords(block, width_dp, lanes, target)

    def core_swap(block):
        return coords(block, lambda x, hi, y, c, q: (x, hi, y, 1 - c, q))

    def x_shift(block, d):
        return coords(block, lambda x, hi, y, c, q: ((x + d) % SIDE, hi, y, c, q))

    def y_shift(block, d):
        return coords(block, lambda x, hi, y, c, q: (x, hi, (y + d) % SIDE, c, q))

    def x_flip(block, bit):
        return coords(block, lambda x, hi, y, c, q: (x ^ bit, hi, y, c, q))

    def y_flip(block, bit):
        return coords(block, lambda x, hi, y, c, q: (x, hi, y ^ bit, c, q))

    def z_flip(block, bit):
        return coords(block, lambda x, hi, y, c, q: (x, hi, y, c, q ^ bit))

    def hi_flip(block):
        return coords(block, lambda x, hi, y, c, q: (x, 1 - hi, y, c, q))

    held, cols = head_weight.shape
    half = held // CORES
    step = (half // SIDE) // 8 * 8
    window = half - (SIDE - 1) * step
    step_y = (cols // SIDE) // 128 * 128
    window_y = cols - (SIDE - 1) * step_y

    def in_order(mine, theirs, bit, axis):
        low = jnp.where(bit == 0, mine, theirs)
        high = jnp.where(bit == 0, theirs, mine)
        return jnp.concatenate([low, high], axis=axis)

    scale = jnp.exp(logit_scale[0])
    bias = logit_bias[0]

    def one_step(stage, *blocks):
        def unused(*_):
            return jax.tree.map(lambda r: jnp.zeros(r.shape, r.dtype), jax.eval_shape(stage, *blocks))

        return lax.cond(scale > 0.0, stage, unused, *blocks)

    def z_shift(block, d):
        def target(x, hi, y, c, q):
            z = (hi * lanes + q + d) % (2 * lanes)
            return x, z // lanes, y, c, z % lanes

        return coords(block, target)

    def gather_z(mine):
        bit = 1
        while 2 * bit < lanes:
            mine = in_order(mine, z_flip(mine, bit), lane // bit % 2, 0)
            bit *= 2
        theirs = jnp.concatenate([z_shift(mine[: bit // 2], bit), z_shift(mine[bit // 2 :], -bit)])
        return in_order(mine, theirs, lane // bit % 2, 0)

    def gather_x(strip):
        pieces = [strip] + [x_shift(strip, d) for d in range(1, SIDE)]
        ours = jnp.zeros((lanes, half, cols), bf16)
        for d, piece in enumerate(pieces):
            ours = lax.dynamic_update_slice_in_dim(ours, piece, (at_x - d) % SIDE * step, 1)
        return in_order(ours, core_swap(ours), core, 1).reshape(lanes * held, cols)

    def sum_xy(total):
        def cut_x(d):
            return lax.dynamic_slice_in_dim(total, (at_x + d) % SIDE * step, window, 1)

        sent = [x_shift(cut_x(d).astype(bf16), d) for d in range(1, SIDE)]
        total_x = cut_x(0)
        for piece in sent:
            total_x = total_x + piece.astype(f32)

        def cut_y(d):
            return lax.dynamic_slice_in_dim(total_x, (at_y + d) % SIDE * step_y, window_y, 2)

        sent = [y_shift(cut_y(d).astype(bf16), d) for d in range(1, SIDE)]
        total_y = cut_y(0)
        for piece in sent:
            total_y = total_y + piece.astype(f32)
        return total_y

    text_f = text_embeds.astype(f32)
    txt_norm = jnp.sqrt(jnp.sum(text_f * text_f, axis=1, keepdims=True) + 1e-06)
    unit_t = text_f / txt_norm
    unit_txt = unit_t.astype(bf16)
    down = [(s, 0, s - 1) for s in range(1, GROUP)]
    up = [(s, 0, s + 1) for s in range(GROUP - 1)]

    ready, unit_txt = lax.optimization_barrier((head_weight, unit_txt))
    mine = lax.dynamic_slice_in_dim(ready, core * half + at_x * step, window, 0)[None]
    mine, moved, near_1 = one_step(
        lambda m: (gather_z(m), chain(unit_txt, [(1, 0, 6)]), chain(unit_txt, down)), mine
    )
    unit_far, mine = lax.optimization_barrier((unit_txt, mine))
    far = chain(unit_far, [(0, -1, 7), (2, -1, 2)])
    far_1 = chain(moved, [(6, -1, 6)])

    def gather_and_chain(mine, near_1):
        near_2 = chain(near_1, down)
        return gather_x(mine), near_2, chain(near_2, down)

    full_weight, near_2, near_3 = one_step(gather_and_chain, mine, near_1)
    full_weight, far, far_1 = lax.optimization_barrier((full_weight, far, far_1))

    projected = jnp.dot(image_features, full_weight, preferred_element_type=f32)
    img_norm = jnp.sqrt(jnp.sum(projected * projected, axis=1, keepdims=True) + 1e-06)
    unit_f = projected / img_norm
    unit_img = unit_f.astype(bf16)

    offset = partner % rows
    ahead = (partner // (rows * lanes) - place) % width_dp
    code = jnp.concatenate([ahead, offset // 128, offset % 128]).astype(bf16)
    code = jnp.pad(code, (0, unit_img.shape[1] - code.shape[0]))
    code = jnp.pad(code[None, :], ((0, 7), (0, 0)))
    parcel = jnp.concatenate([unit_img, code], axis=0)

    offsets = lax.iota(jnp.int32, rows)

    def pair_weight(logits, match):
        sign = jnp.where(match, 1.0, -1.0)
        weights = (-sign * jax.nn.sigmoid(-sign * logits)).astype(bf16)
        return lax.optimization_barrier(weights)

    def met_grad(text, k):
        logits = jnp.einsum("ie,je->ij", unit_img, text, preferred_element_type=f32)
        met = jnp.where(ahead == k, offset, -1)
        weights = pair_weight(scale * logits + bias, met[:, None] == offsets[None, :])
        return scale * jnp.dot(weights, text, preferred_element_type=f32)

    def meet_texts(far, far_1):
        swapped = chain(jnp.where(last, far, far_1), [(7, 0, 6), (6, 0, 7)])
        passed = chain(far, [(2, 0, 7), (7, 0, 5)])
        back_0 = chain(parcel, [(6, 0, 1)])
        beside_1 = chain(parcel, up)
        img_grad = met_grad(unit_txt, 0) + met_grad(jnp.where(last, far, near_1), 1)
        return img_grad, swapped, passed, back_0, beside_1

    def head_terms(img_grad, swapped, passed):
        text_3 = jnp.where(slot >= GROUP - 3, passed, near_3)
        text_3 = jnp.where(slot == GROUP - 2, far_1, text_3)
        img_grad = img_grad + met_grad(jnp.where(slot >= GROUP - 2, swapped, near_2), 2)
        img_grad = img_grad + met_grad(text_3, 3)
        proj_grad = (
            (img_grad - unit_f * jnp.sum(unit_f * img_grad, axis=1, keepdims=True)) / img_norm
        ).astype(bf16)
        term = jnp.einsum(
            "rd,re->de", image_features, proj_grad, preferred_element_type=f32
        ).astype(bf16)
        term = term.reshape(lanes, CORES, half, cols)
        ours = lax.dynamic_index_in_dim(term, core, 1, keepdims=False)
        theirs = lax.dynamic_index_in_dim(term, 1 - core, 1, keepdims=False)
        return ours.astype(f32) + core_swap(theirs).astype(f32)

    def sum_z(total):
        bit = lanes // 2
        while bit:
            halves = total.reshape(2, bit, window, window_y)
            side = lane // bit % 2
            keep = lax.dynamic_index_in_dim(halves, side, 0, keepdims=False)
            give = lax.dynamic_index_in_dim(halves, 1 - side, 0, keepdims=False)
            total = keep + z_flip(give.astype(bf16), bit).astype(f32)
            bit //= 2
        total = total.reshape(window, window_y)
        return (total + hi_flip(total)).astype(bf16)

    img_grad, swapped, passed, back_0, beside_1 = one_step(meet_texts, far, far_1)
    parcel_far, img_grad = lax.optimization_barrier((parcel, img_grad))
    back = chain(parcel_far, [(7, 1, 0), (5, 1, 5)])
    back_1 = chain(back_0, [(1, 1, 1)])

    total = one_step(lambda *blocks: sum_xy(head_terms(*blocks)), img_grad, swapped, passed)
    total, back, back_1 = lax.optimization_barrier((total, back, back_1))

    def sum_z_and_chain(total, back, back_1):
        beside_2 = chain(beside_1, up)
        swapped = chain(jnp.where(first, back, back_1), [(0, 0, 1), (1, 0, 0)])
        passed = chain(back, [(5, 0, 0), (0, 0, 2)])
        return sum_z(total), swapped, passed, beside_2, chain(beside_2, up)

    total_z, swapped, passed, beside_2, beside_3 = one_step(sum_z_and_chain, total, back, back_1)
    parcel, total_z = lax.optimization_barrier((parcel, total_z))
    image_3 = jnp.where(slot <= 2, passed, beside_3)
    images = [
        parcel,
        jnp.where(first, back, beside_1),
        jnp.where(slot <= 1, swapped, beside_2),
        jnp.where(slot == 1, back_1, image_3),
    ]

    strips = total_z[None]
    for bit in (1, 2):
        strips = in_order(strips, y_flip(strips, bit), at_y // bit % 2, 0)
    strip = jnp.concatenate(
        [strips[j, :, :step_y] for j in range(SIDE - 1)] + [strips[SIDE - 1]], axis=1
    )[None]
    for bit in (1, 2):
        strip = in_order(strip, x_flip(strip, bit), at_x // bit % 2, 0)
    ours = jnp.concatenate(
        [strip[j, :step] for j in range(SIDE - 1)] + [strip[SIDE - 1]], axis=0
    )
    head_grad = in_order(ours, core_swap(ours), core, 0).astype(f32)

    txt_grad = 0.0
    for k, image in enumerate(images):
        unit, marks = image[:rows], image[rows].astype(f32).astype(jnp.int32)
        met = marks[rows : 2 * rows] * 128 + marks[2 * rows : 3 * rows]
        met = jnp.where(marks[:rows] == k, met, -1)
        logits = scale * jnp.einsum("je,ie->ji", unit_txt, unit, preferred_element_type=f32) + bias
        weights = pair_weight(logits, met[None, :] == offsets[:, None])
        txt_grad = txt_grad + scale * jnp.dot(weights, unit, preferred_element_type=f32)
    text_grad = (
        (txt_grad - unit_t * jnp.sum(unit_t * txt_grad, axis=1, keepdims=True)) / txt_norm
    ).astype(bf16)
    return (text_grad, head_grad)


def solution(mesh):
    in_specs = (
        P(("dp", "fsdp"), None),
        P("fsdp", None),
        P(("dp", "fsdp"), None),
        P(("dp", "fsdp")),
        P(),
        P(),
    )
    out_specs = (P(("dp", "fsdp"), None), P("fsdp", None))
    return jax.shard_map(
        on_device, mesh=mesh, in_specs=in_specs, out_specs=out_specs, check_vma=False
    )
```

```python
import jax
import jax.numpy as jnp
from jax import lax
from jax.sharding import PartitionSpec as P

STEPS = 4
SIDE = 4
CORES = 2
GROUP = SIDE * CORES
AXES = ("dp", "fsdp")


def along_chain(block, width, lanes, moves):
    groups = width // GROUP
    route = [
        ((g * GROUP + s) * lanes + q, ((g + dg) % groups * GROUP + t) * lanes + q)
        for g in range(groups)
        for q in range(lanes)
        for s, dg, t in moves
    ]
    return lax.ppermute(block, AXES, route)


def by_coords(block, width, lanes, target):
    route = []
    for p in range(width):
        for q in range(lanes):
            x, hi, y, core = p // 16, p // 8 % 2, p // 2 % 4, p % 2
            x2, hi2, y2, core2, q2 = target(x, hi, y, core, q)
            route.append((p * lanes + q, (((x2 * 2 + hi2) * 4 + y2) * 2 + core2) * lanes + q2))
    return lax.ppermute(block, AXES, route)


def on_device(image_features, head_weight, text_embeds, partner, logit_scale, logit_bias):
    bf16, f32 = jnp.bfloat16, jnp.float32
    rows = image_features.shape[0]
    depth = image_features.shape[1]
    width_dp = lax.axis_size("dp")
    lanes = lax.axis_size("fsdp")
    place = lax.axis_index("dp")
    lane = lax.axis_index("fsdp")
    slot = place % GROUP
    core = place % CORES
    at_y = place // CORES % SIDE
    at_x = place // (2 * GROUP)
    first, last = slot == 0, slot == GROUP - 1

    def chain(block, moves):
        return along_chain(block, width_dp, lanes, moves)

    def coords(block, target):
        return by_coords(block, width_dp, lanes, target)

    def core_swap(block):
        return coords(block, lambda x, hi, y, c, q: (x, hi, y, 1 - c, q))

    def x_shift(block, d):
        return coords(block, lambda x, hi, y, c, q: ((x + d) % SIDE, hi, y, c, q))

    def y_shift(block, d):
        return coords(block, lambda x, hi, y, c, q: (x, hi, (y + d) % SIDE, c, q))

    def x_flip(block, bit):
        return coords(block, lambda x, hi, y, c, q: (x ^ bit, hi, y, c, q))

    def y_flip(block, bit):
        return coords(block, lambda x, hi, y, c, q: (x, hi, y ^ bit, c, q))

    def z_flip(block, bit):
        return coords(block, lambda x, hi, y, c, q: (x, hi, y, c, q ^ bit))

    def hi_flip(block):
        return coords(block, lambda x, hi, y, c, q: (x, 1 - hi, y, c, q))

    held, cols = head_weight.shape
    half = held // CORES
    step = (half // SIDE) // 8 * 8
    window = half - (SIDE - 1) * step
    step_y = (cols // SIDE) // 128 * 128
    window_y = cols - (SIDE - 1) * step_y

    def in_order(mine, theirs, bit, axis):
        low = jnp.where(bit == 0, mine, theirs)
        high = jnp.where(bit == 0, theirs, mine)
        return jnp.concatenate([low, high], axis=axis)

    scale = jnp.exp(logit_scale[0])
    bias = logit_bias[0]

    def one_step(stage, *blocks):
        def unused(*_):
            return jax.tree.map(lambda r: jnp.zeros(r.shape, r.dtype), jax.eval_shape(stage, *blocks))

        return lax.cond(scale > 0.0, stage, unused, *blocks)

    LINE = 2

    def on_line(block, d_y, target):
        route = []
        for p in range(width_dp):
            for q in range(lanes):
                x, hi, y, core = p // 16, p // 8 % 2, p // 2 % 4, p % 2
                if y == LINE:
                    hi2, q2 = target(hi, q)
                    p2 = ((x * 2 + hi2) * 4 + (y + d_y) % SIDE) * 2 + core
                    route.append((p * lanes + q, p2 * lanes + q2))
        return lax.ppermute(block, AXES, route)

    def line_shift(block, d):
        def target(hi, q):
            z = (hi * lanes + q + d) % (2 * lanes)
            return z // lanes, z % lanes

        return on_line(block, 0, target)

    def gather_z(mine):
        bit = 1
        while 2 * bit < lanes:
            theirs = on_line(mine, 0, lambda hi, q, bit=bit: (hi, q ^ bit))
            mine = in_order(mine, theirs, lane // bit % 2, 0)
            bit *= 2
        theirs = jnp.concatenate(
            [line_shift(mine[: bit // 2], bit), line_shift(mine[bit // 2 :], -bit)]
        )
        return in_order(mine, theirs, lane // bit % 2, 0)

    def gather_y(strip):
        came = [on_line(strip, d, lambda hi, q: (hi, q)) for d in range(1, SIDE)]
        for d, piece in enumerate(came):
            strip = jnp.where(at_y == (LINE + 1 + d) % SIDE, piece, strip)
        return strip

    def gather_x(strip):
        pieces = [strip] + [x_shift(strip, d) for d in range(1, SIDE)]
        ours = jnp.zeros((lanes, half, cols), bf16)
        for d, piece in enumerate(pieces):
            ours = lax.dynamic_update_slice_in_dim(ours, piece, (at_x - d) % SIDE * step, 1)
        return in_order(ours, core_swap(ours), core, 1).reshape(lanes * held, cols)

    def sum_xy(total):
        def cut_x(d):
            return lax.dynamic_slice_in_dim(total, (at_x + d) % SIDE * step, window, 1)

        sent = [x_shift(cut_x(d).astype(bf16), d) for d in range(1, SIDE)]
        total_x = cut_x(0)
        for piece in sent:
            total_x = total_x + piece.astype(f32)

        def cut_y(d):
            return lax.dynamic_slice_in_dim(total_x, (at_y + d) % SIDE * step_y, window_y, 2)

        sent = [y_shift(cut_y(d).astype(bf16), d) for d in range(1, SIDE)]
        total_y = cut_y(0)
        for piece in sent:
            total_y = total_y + piece.astype(f32)
        return total_y

    text_f = text_embeds.astype(f32)
    txt_norm = jnp.sqrt(jnp.sum(text_f * text_f, axis=1, keepdims=True) + 1e-06)
    unit_t = text_f / txt_norm
    unit_txt = unit_t.astype(bf16)
    down = [(s, 0, s - 1) for s in range(1, GROUP)]
    up = [(s, 0, s + 1) for s in range(GROUP - 1)]

    ready, unit_txt = lax.optimization_barrier((head_weight, unit_txt))
    mine = lax.dynamic_slice_in_dim(ready, core * half + at_x * step, window, 0)[None]
    far = chain(unit_txt, [(0, -1, 7), (2, -1, 2)])

    def along_z(mine):
        moved = chain(unit_txt, [(1, 0, 6)])
        near_1 = chain(unit_txt, down)
        return gather_z(mine), moved, near_1, chain(near_1, down)

    mine, moved, near_1, near_2 = one_step(along_z, mine)
    far_1 = chain(moved, [(6, -1, 6)])
    full_weight = one_step(lambda m: gather_x(gather_y(m)), mine)
    full_weight, far, far_1 = lax.optimization_barrier((full_weight, far, far_1))

    projected = jnp.dot(image_features, full_weight, preferred_element_type=f32)
    img_norm = jnp.sqrt(jnp.sum(projected * projected, axis=1, keepdims=True) + 1e-06)
    unit_f = projected / img_norm
    unit_img = unit_f.astype(bf16)

    offset = partner % rows
    ahead = (partner // (rows * lanes) - place) % width_dp
    code = jnp.concatenate([ahead, offset // 128, offset % 128]).astype(bf16)
    code = jnp.pad(code, (0, unit_img.shape[1] - code.shape[0]))
    code = jnp.pad(code[None, :], ((0, 7), (0, 0)))
    parcel = jnp.concatenate([unit_img, code], axis=0)

    offsets = lax.iota(jnp.int32, rows)

    def pair_weight(logits, match):
        sign = jnp.where(match, 1.0, -1.0)
        weights = (-sign * jax.nn.sigmoid(-sign * logits)).astype(bf16)
        return lax.optimization_barrier(weights)

    def met_grad(text, k):
        logits = jnp.einsum("ie,je->ij", unit_img, text, preferred_element_type=f32)
        met = jnp.where(ahead == k, offset, -1)
        weights = pair_weight(scale * logits + bias, met[:, None] == offsets[None, :])
        return scale * jnp.dot(weights, text, preferred_element_type=f32)

    def meet_texts(far, far_1):
        swapped = chain(jnp.where(last, far, far_1), [(7, 0, 6), (6, 0, 7)])
        passed = chain(far, [(2, 0, 7), (7, 0, 5)])
        back_0 = chain(parcel, [(6, 0, 1)])
        img_grad = met_grad(unit_txt, 0) + met_grad(jnp.where(last, far, near_1), 1)
        return img_grad, swapped, passed, back_0, chain(near_2, down)

    def head_terms(img_grad, swapped, passed, near_3):
        text_3 = jnp.where(slot >= GROUP - 3, passed, near_3)
        text_3 = jnp.where(slot == GROUP - 2, far_1, text_3)
        img_grad = img_grad + met_grad(jnp.where(slot >= GROUP - 2, swapped, near_2), 2)
        img_grad = img_grad + met_grad(text_3, 3)
        proj_grad = (
            (img_grad - unit_f * jnp.sum(unit_f * img_grad, axis=1, keepdims=True)) / img_norm
        ).astype(bf16)
        term = jnp.einsum(
            "rd,re->de", image_features, proj_grad, preferred_element_type=f32
        ).astype(bf16)
        term = term.reshape(lanes, CORES, half, cols)
        ours = lax.dynamic_index_in_dim(term, core, 1, keepdims=False)
        theirs = lax.dynamic_index_in_dim(term, 1 - core, 1, keepdims=False)
        return ours.astype(f32) + core_swap(theirs).astype(f32)

    def sum_z(total, bits):
        for bit in bits:
            halves = total.reshape(2, bit, window, window_y)
            side = lane // bit % 2
            keep = lax.dynamic_index_in_dim(halves, side, 0, keepdims=False)
            give = lax.dynamic_index_in_dim(halves, 1 - side, 0, keepdims=False)
            total = keep + z_flip(give.astype(bf16), bit).astype(f32)
        return total

    bits = [1 << j for j in reversed(range(lanes.bit_length() - 1))]

    img_grad, swapped, passed, back_0, near_3 = one_step(meet_texts, far, far_1)
    parcel_far, img_grad = lax.optimization_barrier((parcel, img_grad))
    back = chain(parcel_far, [(7, 1, 0), (5, 1, 5)])
    back_1 = chain(back_0, [(1, 1, 1)])

    total = one_step(lambda *blocks: sum_xy(head_terms(*blocks)), img_grad, swapped, passed, near_3)
    total, back, back_1, parcel_near = lax.optimization_barrier((total, back, back_1, parcel))

    def sum_z_and_chain(total, back, back_1):
        swapped = chain(jnp.where(first, back, back_1), [(0, 0, 1), (1, 0, 0)])
        passed = chain(back, [(5, 0, 0), (0, 0, 2)])
        return sum_z(total, bits[:-1]), swapped, passed

    def sum_z_last(total, beside_1):
        total = sum_z(total, bits[-1:]).reshape(window, window_y)
        return (total + hi_flip(total)).astype(bf16), chain(beside_1, up)

    beside_1 = chain(parcel_near, up)
    total, swapped, passed = one_step(sum_z_and_chain, total, back, back_1)
    total, beside_1 = lax.optimization_barrier((total, beside_1))
    total_z, beside_2 = one_step(sum_z_last, total, beside_1)
    beside_3 = chain(beside_2, up)
    parcel, total_z = lax.optimization_barrier((parcel, total_z))
    image_3 = jnp.where(slot <= 2, passed, beside_3)
    images = [
        parcel,
        jnp.where(first, back, beside_1),
        jnp.where(slot <= 1, swapped, beside_2),
        jnp.where(slot == 1, back_1, image_3),
    ]

    strips = total_z[None]
    for bit in (1, 2):
        strips = in_order(strips, y_flip(strips, bit), at_y // bit % 2, 0)
    strip = jnp.concatenate(
        [strips[j, :, :step_y] for j in range(SIDE - 1)] + [strips[SIDE - 1]], axis=1
    )[None]
    for bit in (1, 2):
        strip = in_order(strip, x_flip(strip, bit), at_x // bit % 2, 0)
    ours = jnp.concatenate(
        [strip[j, :step] for j in range(SIDE - 1)] + [strip[SIDE - 1]], axis=0
    )
    head_grad = in_order(ours, core_swap(ours), core, 0).astype(f32)

    txt_grad = 0.0
    for k, image in enumerate(images):
        unit, marks = image[:rows], image[rows].astype(f32).astype(jnp.int32)
        met = marks[rows : 2 * rows] * 128 + marks[2 * rows : 3 * rows]
        met = jnp.where(marks[:rows] == k, met, -1)
        logits = scale * jnp.einsum("je,ie->ji", unit_txt, unit, preferred_element_type=f32) + bias
        weights = pair_weight(logits, met[None, :] == offsets[:, None])
        txt_grad = txt_grad + scale * jnp.dot(weights, unit, preferred_element_type=f32)
    text_grad = (
        (txt_grad - unit_t * jnp.sum(unit_t * txt_grad, axis=1, keepdims=True)) / txt_norm
    ).astype(bf16)
    return (text_grad, head_grad)


def solution(mesh):
    in_specs = (
        P(("dp", "fsdp"), None),
        P("fsdp", None),
        P(("dp", "fsdp"), None),
        P(("dp", "fsdp")),
        P(),
        P(),
    )
    out_specs = (P(("dp", "fsdp"), None), P("fsdp", None))
    return jax.shard_map(
        on_device, mesh=mesh, in_specs=in_specs, out_specs=out_specs, check_vma=False
    )
```

```python
import jax
import jax.numpy as jnp
from jax import lax
from jax.sharding import PartitionSpec as P

STEPS = 4
SIDE = 4
CORES = 2
GROUP = SIDE * CORES
AXES = ("dp", "fsdp")


def along_chain(block, width, lanes, moves):
    groups = width // GROUP
    route = [
        ((g * GROUP + s) * lanes + q, ((g + dg) % groups * GROUP + t) * lanes + q)
        for g in range(groups)
        for q in range(lanes)
        for s, dg, t in moves
    ]
    return lax.ppermute(block, AXES, route)


def by_coords(block, width, lanes, target):
    route = []
    for p in range(width):
        for q in range(lanes):
            x, hi, y, core = p // 16, p // 8 % 2, p // 2 % 4, p % 2
            x2, hi2, y2, core2, q2 = target(x, hi, y, core, q)
            route.append((p * lanes + q, (((x2 * 2 + hi2) * 4 + y2) * 2 + core2) * lanes + q2))
    return lax.ppermute(block, AXES, route)


def on_device(image_features, head_weight, text_embeds, partner, logit_scale, logit_bias):
    bf16, f32 = jnp.bfloat16, jnp.float32
    rows = image_features.shape[0]
    depth = image_features.shape[1]
    width_dp = lax.axis_size("dp")
    lanes = lax.axis_size("fsdp")
    place = lax.axis_index("dp")
    lane = lax.axis_index("fsdp")
    slot = place % GROUP
    core = place % CORES
    at_y = place // CORES % SIDE
    at_x = place // (2 * GROUP)
    first, last = slot == 0, slot == GROUP - 1

    def chain(block, moves):
        return along_chain(block, width_dp, lanes, moves)

    def coords(block, target):
        return by_coords(block, width_dp, lanes, target)

    def core_swap(block):
        return coords(block, lambda x, hi, y, c, q: (x, hi, y, 1 - c, q))

    def x_shift(block, d):
        return coords(block, lambda x, hi, y, c, q: ((x + d) % SIDE, hi, y, c, q))

    def y_shift(block, d):
        return coords(block, lambda x, hi, y, c, q: (x, hi, (y + d) % SIDE, c, q))

    def x_flip(block, bit):
        return coords(block, lambda x, hi, y, c, q: (x ^ bit, hi, y, c, q))

    def y_flip(block, bit):
        return coords(block, lambda x, hi, y, c, q: (x, hi, y ^ bit, c, q))

    def z_flip(block, bit):
        return coords(block, lambda x, hi, y, c, q: (x, hi, y, c, q ^ bit))

    def hi_flip(block):
        return coords(block, lambda x, hi, y, c, q: (x, 1 - hi, y, c, q))

    held, cols = head_weight.shape
    half = held // CORES
    step = (half // SIDE) // 8 * 8
    window = half - (SIDE - 1) * step
    step_y = (cols // SIDE) // 128 * 128
    window_y = cols - (SIDE - 1) * step_y

    def in_order(mine, theirs, bit, axis):
        low = jnp.where(bit == 0, mine, theirs)
        high = jnp.where(bit == 0, theirs, mine)
        return jnp.concatenate([low, high], axis=axis)

    scale = jnp.exp(logit_scale[0])
    bias = logit_bias[0]

    def one_step(stage, *blocks):
        def unused(*_):
            return jax.tree.map(lambda r: jnp.zeros(r.shape, r.dtype), jax.eval_shape(stage, *blocks))

        return lax.cond(scale > 0.0, stage, unused, *blocks)

    def z_shift(block, d):
        def target(x, hi, y, c, q):
            z = (hi * lanes + q + d) % (2 * lanes)
            return x, z // lanes, y, c, z % lanes

        return coords(block, target)

    def gather_z(mine):
        bit = 1
        while 2 * bit < lanes:
            mine = in_order(mine, z_flip(mine, bit), lane // bit % 2, 0)
            bit *= 2
        theirs = jnp.concatenate([z_shift(mine[: bit // 2], bit), z_shift(mine[bit // 2 :], -bit)])
        return in_order(mine, theirs, lane // bit % 2, 0)

    def gather_x(strip):
        pieces = [strip] + [x_shift(strip, d) for d in range(1, SIDE)]
        ours = jnp.zeros((lanes, half, cols), bf16)
        for d, piece in enumerate(pieces):
            ours = lax.dynamic_update_slice_in_dim(ours, piece, (at_x - d) % SIDE * step, 1)
        return in_order(ours, core_swap(ours), core, 1).reshape(lanes * held, cols)

    def sum_xy(total):
        def cut_x(d):
            return lax.dynamic_slice_in_dim(total, (at_x + d) % SIDE * step, window, 1)

        sent = [x_shift(cut_x(d).astype(bf16), d) for d in range(1, SIDE)]
        total_x = cut_x(0)
        for piece in sent:
            total_x = total_x + piece.astype(f32)

        def cut_y(d):
            return lax.dynamic_slice_in_dim(total_x, (at_y + d) % SIDE * step_y, window_y, 2)

        sent = [y_shift(cut_y(d).astype(bf16), d) for d in range(1, SIDE)]
        total_y = cut_y(0)
        for piece in sent:
            total_y = total_y + piece.astype(f32)
        return total_y

    text_f = text_embeds.astype(f32)
    txt_norm = jnp.sqrt(jnp.sum(text_f * text_f, axis=1, keepdims=True) + 1e-06)
    unit_t = text_f / txt_norm
    unit_txt = unit_t.astype(bf16)
    down = [(s, 0, s - 1) for s in range(1, GROUP)]
    up = [(s, 0, s + 1) for s in range(GROUP - 1)]

    ready, unit_txt = lax.optimization_barrier((head_weight, unit_txt))
    mine = lax.dynamic_slice_in_dim(ready, core * half + at_x * step, window, 0)[None]
    mine, moved, near_1 = one_step(
        lambda m: (gather_z(m), chain(unit_txt, [(1, 0, 6)]), chain(unit_txt, down)), mine
    )
    unit_far, mine = lax.optimization_barrier((unit_txt, mine))
    far = chain(unit_far, [(0, -1, 7), (2, -1, 2)])
    far_1 = chain(moved, [(6, -1, 6)])

    def gather_and_chain(mine, near_1):
        near_2 = chain(near_1, down)
        return gather_x(mine), near_2, chain(near_2, down)

    full_weight, near_2, near_3 = one_step(gather_and_chain, mine, near_1)
    full_weight, far, far_1 = lax.optimization_barrier((full_weight, far, far_1))

    projected = jnp.dot(image_features, full_weight, preferred_element_type=f32)
    img_norm = jnp.sqrt(jnp.sum(projected * projected, axis=1, keepdims=True) + 1e-06)
    unit_f = projected / img_norm
    unit_img = unit_f.astype(bf16)

    offset = partner % rows
    ahead = (partner // (rows * lanes) - place) % width_dp
    code = jnp.concatenate([ahead, offset // 128, offset % 128]).astype(bf16)
    code = jnp.pad(code, (0, unit_img.shape[1] - code.shape[0]))
    code = jnp.pad(code[None, :], ((0, 7), (0, 0)))
    parcel = jnp.concatenate([unit_img, code], axis=0)

    offsets = lax.iota(jnp.int32, rows)

    def pair_weight(logits, match):
        sign = jnp.where(match, 1.0, -1.0)
        weights = (-sign * jax.nn.sigmoid(-sign * logits)).astype(bf16)
        return lax.optimization_barrier(weights)

    def met_grad(text, k):
        logits = jnp.einsum("ie,je->ij", unit_img, text, preferred_element_type=f32)
        met = jnp.where(ahead == k, offset, -1)
        weights = pair_weight(scale * logits + bias, met[:, None] == offsets[None, :])
        return scale * jnp.dot(weights, text, preferred_element_type=f32)

    def meet_texts(far, far_1):
        swapped = chain(jnp.where(last, far, far_1), [(7, 0, 6), (6, 0, 7)])
        passed = chain(far, [(2, 0, 7), (7, 0, 5)])
        swapped, passed = lax.optimization_barrier((swapped, passed))
        img_grad = met_grad(unit_txt, 0) + met_grad(jnp.where(last, far, near_1), 1)
        return img_grad, swapped, passed

    def head_terms(img_grad, swapped, passed):
        text_3 = jnp.where(slot >= GROUP - 3, passed, near_3)
        text_3 = jnp.where(slot == GROUP - 2, far_1, text_3)
        img_grad = img_grad + met_grad(jnp.where(slot >= GROUP - 2, swapped, near_2), 2)
        img_grad = img_grad + met_grad(text_3, 3)
        proj_grad = (
            (img_grad - unit_f * jnp.sum(unit_f * img_grad, axis=1, keepdims=True)) / img_norm
        ).astype(bf16)
        term = jnp.einsum(
            "rd,re->de", image_features, proj_grad, preferred_element_type=f32
        ).astype(bf16)
        term = term.reshape(lanes, CORES, half, cols)
        ours = lax.dynamic_index_in_dim(term, core, 1, keepdims=False)
        theirs = lax.dynamic_index_in_dim(term, 1 - core, 1, keepdims=False)
        return ours.astype(f32) + core_swap(theirs).astype(f32)

    def sum_z(total):
        bit = lanes // 2
        while bit:
            halves = total.reshape(2, bit, window, window_y)
            side = lane // bit % 2
            keep = lax.dynamic_index_in_dim(halves, side, 0, keepdims=False)
            give = lax.dynamic_index_in_dim(halves, 1 - side, 0, keepdims=False)
            total = keep + z_flip(give.astype(bf16), bit).astype(f32)
            bit //= 2
        total = total.reshape(window, window_y)
        return (total + hi_flip(total)).astype(bf16)

    back = chain(parcel, [(7, 1, 7), (5, 1, 5), (6, 0, 0)])
    total = one_step(lambda *blocks: head_terms(*meet_texts(*blocks)), far, far_1)
    total, back, parcel = lax.optimization_barrier((total, back, parcel))
    back_2 = chain(back, [(0, 1, 0), (5, 0, 7)])
    image_1 = chain(jnp.where(last, back, parcel), up + [(7, 0, 0)])
    total = one_step(sum_xy, total)
    total, back_2, image_1 = lax.optimization_barrier((total, back_2, image_1))
    come_2 = chain(jnp.where(last, back_2, image_1), up + [(7, 0, 0)])
    total_z = one_step(sum_z, total)
    total_z, come_2, parcel = lax.optimization_barrier((total_z, come_2, parcel))
    image_2 = jnp.where(first, back_2, come_2)
    come_3 = chain(image_2, up)
    images = [parcel, image_1, image_2, jnp.where(first, come_2, come_3)]

    strips = total_z[None]
    for bit in (1, 2):
        strips = in_order(strips, y_flip(strips, bit), at_y // bit % 2, 0)
    strip = jnp.concatenate(
        [strips[j, :, :step_y] for j in range(SIDE - 1)] + [strips[SIDE - 1]], axis=1
    )[None]
    for bit in (1, 2):
        strip = in_order(strip, x_flip(strip, bit), at_x // bit % 2, 0)
    ours = jnp.concatenate(
        [strip[j, :step] for j in range(SIDE - 1)] + [strip[SIDE - 1]], axis=0
    )
    head_grad = in_order(ours, core_swap(ours), core, 0).astype(f32)

    txt_grad = 0.0
    for k, image in enumerate(images):
        unit, marks = image[:rows], image[rows].astype(f32).astype(jnp.int32)
        met = marks[rows : 2 * rows] * 128 + marks[2 * rows : 3 * rows]
        met = jnp.where(marks[:rows] == k, met, -1)
        logits = scale * jnp.einsum("je,ie->ji", unit_txt, unit, preferred_element_type=f32) + bias
        weights = pair_weight(logits, met[None, :] == offsets[:, None])
        txt_grad = txt_grad + scale * jnp.dot(weights, unit, preferred_element_type=f32)
    text_grad = (
        (txt_grad - unit_t * jnp.sum(unit_t * txt_grad, axis=1, keepdims=True)) / txt_norm
    ).astype(bf16)
    return (text_grad, head_grad)


def solution(mesh):
    in_specs = (
        P(("dp", "fsdp"), None),
        P("fsdp", None),
        P(("dp", "fsdp"), None),
        P(("dp", "fsdp")),
        P(),
        P(),
    )
    out_specs = (P(("dp", "fsdp"), None), P("fsdp", None))
    return jax.shard_map(
        on_device, mesh=mesh, in_specs=in_specs, out_specs=out_specs, check_vma=False
    )
```
